32 devices in a mesh: kx: 4 (over y, x), ky: 8 (over z, core).
Axes of the slice: x: 2, y: 2, z: 4, core: 2. Of those that a mesh axis runs over, the one named last changes fastest.
Arguments:
- states: bfloat16 [32, 4096, 128], P(('kx', 'ky')), may hold values from -6 to 6
- energies: bfloat16 [32, 128], P(('kx', 'ky')), may hold values from -2 to 2
- external: float32 [1, 4096], replicated, may hold values from -6 to 6
- reorder: int32 [2, 32, 4096], P(None, ('kx', 'ky')), may hold values from 0 to 4095, each once within a row
Outputs:
- band_response: float32 [32, 2, 1, 128, 128], P(('kx', 'ky'))
- density: float32 [2, 1, 4096], replicated
The draws below stay inside these ranges and needn't reach their ends.
Inputs may be any that keep to these rules, and one draw needn't show every extreme that they name: Each row reorder[q, k] is a permutation of the 4096 grid components.
All inputs are finite; a program needn't handle non-finite values.
Results may differ from the reference program's by a relative error of at most 0.0029.
Values may be sent and summed in bfloat16 or wider, within the bound.
A program may use at most 64 MiB of HBM per device.

```python
import math
import jax
import jax.numpy as jnp
from jax import lax

GX = 64
GY = 64
NB = 128
NQ = 2
NDIR = 1
ITERS = 2
G = 4096
K = 32
N_KX = 4
N_KY = 8


def levels(own_key, shape, shards, smallest, largest):
    def one(dim, parts):
        steps = jax.random.uniform(jax.random.fold_in(jax.random.fold_in(own_key, 6), dim), (parts,), jnp.float32, smallest / len(shards), largest / len(shards))
        return jnp.repeat(jnp.exp(steps), shape[dim] // parts).reshape((-1,) + (1,) * (len(shape) - dim - 1))

    loudness = one(*shards[0])
    for cut in shards[1:]:
        loudness = loudness * one(*cut)
    return loudness


def noise(stream_key, extent, spread, bound, shards=(), kind=jnp.bfloat16):
    values = jax.random.normal(stream_key, extent, jnp.float32) * spread
    if len(shards) > 0:
        values = levels(stream_key, extent, shards, -0.22, 0.18) * values
    return jnp.clip(values, min=-bound, max=bound).astype(kind)


def setup_inputs(seed: int = 0) -> dict:
    splits = jax.random.split(jax.random.key(seed), 5)
    return {
        "states": noise(splits[0], (K, G, NB), 1.0, 6.0, ((0, 32),)),
        "energies": jnp.clip(jax.random.uniform(splits[1], (K, NB), jnp.float32, -2.0, 2.0) * levels(splits[1], (K, NB), ((0, 32),), -0.4, 0.0), -2.0, 2.0).astype(jnp.bfloat16),
        "external": noise(splits[2], (NDIR, G), 1.0, 6.0, (), jnp.float32),
        "reorder": jax.vmap(lambda own: jax.random.permutation(own, G))(jax.random.split(splits[3], NQ * K)).reshape((NQ, K, G)).astype(jnp.int32),
    }


SMEAR = 0.5
FERMI = 0.0
SCREEN = 4.0

def hartley_table(length):
    positions = jnp.arange(length, dtype=jnp.int32)
    phases = positions[:, None] * positions[None, :] % length
    angles = phases.astype(jnp.float32) * (2.0 * math.pi / length)
    return (jnp.cos(angles) + jnp.sin(angles)) / math.sqrt(length)

def screening(len_x, len_y):
    freq_x = jnp.arange(len_x, dtype=jnp.int32)
    freq_x = jnp.minimum(freq_x, len_x - freq_x).astype(jnp.float32)
    freq_y = jnp.arange(len_y, dtype=jnp.int32)
    freq_y = jnp.minimum(freq_y, len_y - freq_y).astype(jnp.float32)
    return 1.0 / (1.0 + (freq_x[:, None] ** 2 + freq_y[None, :] ** 2) / SCREEN)

def coulomb(density):
    fields = density.reshape(density.shape[:-1] + (GX, GY))
    table_x = hartley_table(GX)
    table_y = hartley_table(GY)
    spectra = jnp.einsum('pi,abij,jq->abpq', table_x, fields, table_y, precision=lax.Precision.HIGHEST)
    spectra = spectra * screening(GX, GY)
    result = jnp.einsum('pi,abij,jq->abpq', table_x, spectra, table_y, precision=lax.Precision.HIGHEST)
    return result.reshape(density.shape)

def occupation(energy):
    return 1.0 / (1.0 + jnp.exp((energy - FERMI) / SMEAR))

def respond(orbital, energy, far_states, far_energy, potential):
    orbital_wide = orbital.astype(jnp.float32)
    far_wide = far_states.astype(jnp.float32)
    energy = energy.astype(jnp.float32)
    far_energy = far_energy.astype(jnp.float32)
    weighted = (potential[:, :, None] * orbital_wide[None]).astype(jnp.bfloat16).astype(jnp.float32)
    band_mats = jnp.einsum('gm,agn->amn', far_wide, weighted, precision=lax.Precision.HIGHEST)
    band_mats = band_mats * (1.0 / math.sqrt(orbital.shape[0]))
    gap_matrix = far_energy[:, None] - energy[None, :]
    weight = (occupation(energy)[None, :] - occupation(far_energy)[:, None]) * gap_matrix / (gap_matrix * gap_matrix + SMEAR * SMEAR)
    response = weight[None] * band_mats
    response_low = response.astype(jnp.bfloat16).astype(jnp.float32)
    orbitals_out = jnp.einsum('gm,amn->agn', far_wide, response_low, precision=lax.Precision.HIGHEST)
    orbitals_out = orbitals_out * (1.0 / math.sqrt(orbital.shape[1]))
    contrib = lax.optimization_barrier(jnp.sum(orbital_wide[None] * orbitals_out, axis=2))
    return (response, contrib)

def reference(states, energies, external, reorder):
    potential = jnp.broadcast_to(external[None], (NQ, NDIR, G))

    def per_point(kpoint, potential):
        orbital = states[kpoint]
        energy = energies[kpoint]
        row_index = kpoint // N_KY
        col_index = kpoint % N_KY
        partners = [(row_index + 1) % N_KX * N_KY + col_index, row_index * N_KY + (col_index + 1) % N_KY]
        responses = []
        contribs = []
        for q_index in range(NQ):
            partner = partners[q_index]
            far_states = jnp.take(states[partner], reorder[q_index, kpoint], axis=0)
            response, contrib = respond(orbital, energy, far_states, energies[partner], potential[q_index])
            responses.append(response)
            contribs.append(contrib)
        return (jnp.stack(responses), jnp.stack(contribs))
    kpoints = jnp.arange(K, dtype=jnp.int32)
    for rounds in range(ITERS):
        band_response, contribs = lax.map(lambda kpoint: per_point(kpoint, potential), kpoints)
        density = lax.optimization_barrier(jnp.sum(contribs, axis=0)) * (1.0 / math.sqrt(K))
        if rounds + 1 < ITERS:
            potential = external[None] + coulomb(density)
    return (band_response, density)
```

```python
import functools
import math

import jax
import jax.numpy as jnp
import numpy as np
from jax import lax
from jax.experimental import pallas as pl
from jax.experimental.pallas import tpu as pltpu
from jax.sharding import PartitionSpec as P

GX = 64
ITERS = 2


SMEAR = 0.5
FERMI = 0.0
SCREEN = 4.0
PIECES = 8
ROWS = 32
MESH = pl.DeviceIdType.MESH


def hartley_table(length):
    positions = np.arange(length)
    angles = (positions[:, None] * positions[None, :] % length) * (2.0 * math.pi / length)
    return ((np.cos(angles) + np.sin(angles)) / math.sqrt(length)).astype(np.float32)


def screening(len_x, len_y):
    freq_x = np.arange(len_x)
    freq_x = np.minimum(freq_x, len_x - freq_x).astype(np.float32)
    freq_y = np.arange(len_y)
    freq_y = np.minimum(freq_y, len_y - freq_y).astype(np.float32)
    return 1.0 / (1.0 + (freq_x[:, None] ** 2 + freq_y[None, :] ** 2) / SCREEN)


def occupation(energy):
    return 1.0 / (1.0 + jnp.exp((energy - FERMI) / SMEAR))


def kernel(
    n_kx,
    n_ky,
    states,
    energy,
    reorder,
    external,
    table_x,
    table_y,
    screen,
    response_out,
    density_out,
    wide,
    stage,
    outgoing,
    far,
    far_energy,
    wanted,
    order,
    weighted,
    part,
    gathered,
    crossed,
    whole,
    order_send,
    order_recv,
    order_local,
    energy_send,
    energy_recv,
    rows_send,
    rows_recv,
    sum_send,
    sum_recv,
    cross_send,
    cross_recv,
    spread_send,
    spread_recv,
):
    grid, bands = states.shape
    nq = reorder.shape[0]
    len_y = grid // GX
    piece = grid // PIECES
    columns = GX // PIECES
    kx = lax.axis_index("kx")
    ky = lax.axis_index("ky")

    def remote(source, target, send, recv, where):
        return pltpu.make_async_remote_copy(
            src_ref=source, dst_ref=target, send_sem=send, recv_sem=recv, device_id=where, device_id_type=MESH
        )

    barrier = pltpu.get_barrier_semaphore()
    for step in range(1, n_kx):
        pl.semaphore_signal(barrier, inc=1, device_id={"kx": lax.rem(kx + step, n_kx)}, device_id_type=MESH)
    for step in range(1, n_ky):
        pl.semaphore_signal(barrier, inc=1, device_id={"ky": lax.rem(ky + step, n_ky)}, device_id_type=MESH)
    wide[...] = states[...].astype(jnp.float32)
    pl.semaphore_wait(barrier, n_kx + n_ky - 2)

    ahead = ({"kx": lax.rem(kx + 1, n_kx)}, {"ky": lax.rem(ky + 1, n_ky)})
    behind = ({"kx": lax.rem(kx + n_kx - 1, n_kx)}, {"ky": lax.rem(ky + n_ky - 1, n_ky)})

    orders = [
        remote(reorder.at[q], wanted.at[q], order_send.at[q], order_recv.at[q], ahead[q]) for q in range(nq)
    ]
    energies = [
        remote(energy, far_energy.at[q], energy_send.at[q], energy_recv.at[q], behind[q]) for q in range(nq)
    ]
    for q in range(nq):
        orders[q].start()
    for q in range(nq):
        energies[q].start()
    locals_ = [pltpu.make_async_copy(wanted.at[q], order.at[q], order_local.at[q]) for q in range(nq)]
    for q in range(nq):
        orders[q].wait_recv()
        locals_[q].start()
    for q in range(nq):
        locals_[q].wait()

    def rows_copy(q, c):
        rows = pl.ds(pl.multiple_of(c * piece, piece), piece)
        return remote(
            outgoing.at[q, rows], far.at[q, rows], rows_send.at[q, c], rows_recv.at[q, c], behind[q]
        )

    def send_piece(c, carry):
        for q in range(nq):

            def some_rows(b, inner):
                first = pl.multiple_of(c * piece + b * ROWS, ROWS)
                for half in range(0, ROWS, 16):
                    picked = [wide[pl.ds(order[q, 0, first + half + r], 1), :] for r in range(16)]
                    for r in range(16):
                        stage[half + r : half + r + 1, :] = picked[r]
                outgoing[q, pl.ds(first, ROWS), :] = stage[...].astype(jnp.bfloat16)
                return inner

            lax.fori_loop(0, piece // ROWS, some_rows, 0)
            rows_copy(q, c).start()
        return carry

    lax.fori_loop(0, PIECES, send_piece, 0)

    own = energy[0:1, :]
    weights = []
    for q in range(nq):
        energies[q].wait_recv()
        other = jnp.broadcast_to(far_energy[q, 0:1, :], (bands, bands)).T
        gap = other - own
        weights.append((occupation(own) - occupation(other)) * gap / (gap * gap + SMEAR * SMEAR))

    lanes = lax.broadcasted_iota(jnp.int32, (len_y, nq * GX), 1)

    def bands_of(q, potential, waits):
        def one(c, total):
            if waits:
                rows_copy(q, c).wait_recv()
            turned = pltpu.roll(potential, lax.rem(2 * nq * GX - q * GX - c * columns, nq * GX), 1)
            for x in range(columns):
                rows = pl.ds(pl.multiple_of(c * piece + x * len_y, len_y), len_y)
                scaled = turned[:, x : x + 1] * states[rows, :].astype(jnp.float32)
                weighted[x * len_y : (x + 1) * len_y, :] = scaled.astype(jnp.bfloat16)
            rows = pl.ds(pl.multiple_of(c * piece, piece), piece)
            return total + lax.dot_general(
                far[q, rows, :],
                weighted[...],
                (((0,), (0,)), ((), ())),
                preferred_element_type=jnp.float32,
            )

        return lax.fori_loop(0, PIECES, one, jnp.zeros((bands, bands), jnp.float32))

    def density_of(q, low, total):
        def one(c, total):
            rows = pl.ds(pl.multiple_of(c * piece, piece), piece)
            out = jnp.dot(far[q, rows, :], low, preferred_element_type=jnp.float32)
            out = out * states[rows, :].astype(jnp.float32)
            for x in range(columns):
                column = jnp.sum(out[x * len_y : (x + 1) * len_y, :], axis=1, keepdims=True)
                total = jnp.where(lanes == q * GX + c * columns + x, column, total)
            return total

        return lax.fori_loop(0, PIECES, one, total)

    scale = 1.0 / (math.sqrt(bands) * math.sqrt(n_kx * n_ky))

    def summed(rnd, total):
        part[rnd] = total.reshape(part.shape[1:])
        sends = []
        for d in range(1, n_ky):
            target = lax.rem(ky + d, n_ky)
            sends.append(
                remote(
                    part.at[rnd, target],
                    gathered.at[rnd, d],
                    sum_send.at[rnd, d],
                    sum_recv.at[rnd, d],
                    {"ky": target},
                )
            )
        for copy in sends:
            copy.start()
        mine = part[rnd, ky]
        for d, copy in enumerate(sends):
            copy.wait_recv()
            mine = mine + gathered[rnd, d + 1]
        crossed[rnd, kx] = mine
        crosses = []
        for d in range(1, n_kx):
            crosses.append(
                remote(
                    crossed.at[rnd, kx],
                    crossed.at[rnd, kx],
                    cross_send.at[rnd, d],
                    cross_recv.at[rnd, d],
                    {"kx": lax.rem(kx + d, n_kx)},
                )
            )
        for copy in crosses:
            copy.start()
        for copy in crosses:
            copy.wait_recv()
        mine = crossed[rnd, 0]
        for d in range(1, n_kx):
            mine = mine + crossed[rnd, d]
        whole[rnd, ky] = mine * scale
        spreads = []
        for d in range(1, n_ky):
            spreads.append(
                remote(
                    whole.at[rnd, ky],
                    whole.at[rnd, ky],
                    spread_send.at[rnd, d],
                    spread_recv.at[rnd, d],
                    {"ky": lax.rem(ky + d, n_ky)},
                )
            )
        for copy in spreads:
            copy.start()
        for copy in spreads:
            copy.wait_recv()
        return whole[rnd].reshape(total.shape), sends + crosses + spreads

    def exact(left, right):
        return jnp.dot(left, right, preferred_element_type=jnp.float32, precision=lax.Precision.HIGHEST)

    potential = external[...]
    pending = []
    for rnd in range(ITERS):
        total = jnp.zeros((len_y, nq * GX), jnp.float32)
        for q in reversed(range(nq)):
            mats = bands_of(q, potential, rnd == 0) * (1.0 / math.sqrt(grid))
            response = weights[q] * mats
            if rnd + 1 == ITERS:
                response_out[q] = response
            total = density_of(q, response.astype(jnp.bfloat16), total)
        density, sends = summed(rnd, total)
        pending = pending + sends
        if rnd + 1 < ITERS:
            spectrum = exact(exact(table_y[...], density), table_x[...]) * screen[...]
            potential = external[...] + exact(exact(table_y[...], spectrum), table_x[...])
    density_out[...] = density

    for q in range(nq):
        orders[q].wait_send()
        energies[q].wait_send()

    def drain(c, carry):
        for q in range(nq):
            rows_copy(q, c).wait_send()
        return carry

    lax.fori_loop(0, PIECES, drain, 0)
    for copy in pending:
        copy.wait_send()


def shards(n_kx, n_ky, states, energies, external, reorder):
    orbital = states[0]
    grid, bands = orbital.shape
    nq = reorder.shape[0]
    len_y = grid // GX
    energy = jnp.broadcast_to(energies.astype(jnp.float32), (8, bands))
    bare = jnp.tile(external.reshape(GX, len_y).T, (1, nq))
    table_x = jnp.asarray(np.kron(np.eye(nq, dtype=np.float32), hartley_table(GX)))
    table_y = jnp.asarray(hartley_table(len_y))
    screen = jnp.asarray(np.tile(screening(GX, len_y).T, (1, nq)).astype(np.float32))
    tall = len_y // n_ky
    wide = nq * GX
    vmem = pl.BlockSpec(memory_space=pltpu.VMEM)
    dma = pltpu.SemaphoreType.DMA
    response, density = pl.pallas_call(
        functools.partial(kernel, n_kx, n_ky),
        out_shape=(
            jax.ShapeDtypeStruct((nq, bands, bands), jnp.float32),
            jax.ShapeDtypeStruct((len_y, wide), jnp.float32),
        ),
        in_specs=[vmem, vmem, vmem, vmem, vmem, vmem, vmem],
        out_specs=(vmem, vmem),
        scratch_shapes=[
            pltpu.VMEM((grid, bands), jnp.float32),
            pltpu.VMEM((ROWS, bands), jnp.float32),
            pltpu.VMEM((nq, grid, bands), jnp.bfloat16),
            pltpu.VMEM((nq, grid, bands), jnp.bfloat16),
            pltpu.VMEM((nq, 8, bands), jnp.float32),
            pltpu.VMEM((nq, 1, grid), jnp.int32),
            pltpu.SMEM((nq, 1, grid), jnp.int32),
            pltpu.VMEM((grid // PIECES, bands), jnp.bfloat16),
            pltpu.VMEM((ITERS, n_ky, tall, wide), jnp.float32),
            pltpu.VMEM((ITERS, n_ky, tall, wide), jnp.float32),
            pltpu.VMEM((ITERS, n_kx, tall, wide), jnp.float32),
            pltpu.VMEM((ITERS, n_ky, tall, wide), jnp.float32),
            dma((nq,)),
            dma((nq,)),
            dma((nq,)),
            dma((nq,)),
            dma((nq,)),
            dma((nq, PIECES)),
            dma((nq, PIECES)),
            dma((ITERS, n_ky)),
            dma((ITERS, n_ky)),
            dma((ITERS, n_kx)),
            dma((ITERS, n_kx)),
            dma((ITERS, n_ky)),
            dma((ITERS, n_ky)),
        ],
        compiler_params=pltpu.CompilerParams(
            collective_id=0, has_side_effects=True, vmem_limit_bytes=40 * 2**20
        ),
        cost_estimate=pl.CostEstimate(flops=2**31, bytes_accessed=2**23, transcendentals=2**16),
    )(orbital, energy, reorder, bare, table_x, table_y, screen)
    density = density.reshape(len_y, nq, GX).transpose(1, 2, 0).reshape(nq, 1, grid)
    return (response[None, :, None], density)


def solution(mesh):
    return jax.shard_map(
        functools.partial(shards, mesh.shape["kx"], mesh.shape["ky"]),
        mesh=mesh,
        in_specs=(
            P(("kx", "ky"), None, None),
            P(("kx", "ky"), None),
            P(),
            P(None, ("kx", "ky"), None),
        ),
        out_specs=(P(("kx", "ky"), None, None, None, None), P()),
        check_vma=False,
    )
```

```python
import functools
import math

import jax
import jax.numpy as jnp
import numpy as np
from jax import lax
from jax.experimental import pallas as pl
from jax.experimental.pallas import tpu as pltpu
from jax.sharding import PartitionSpec as P

GX = 64
ITERS = 2


SMEAR = 0.5
FERMI = 0.0
SCREEN = 4.0
PIECES = 8
ROWS = 32
LANES = 128
MESH = pl.DeviceIdType.MESH


def hartley_table(length):
    positions = np.arange(length)
    angles = (positions[:, None] * positions[None, :] % length) * (2.0 * math.pi / length)
    return ((np.cos(angles) + np.sin(angles)) / math.sqrt(length)).astype(np.float32)


def screening(len_x, len_y):
    freq_x = np.arange(len_x)
    freq_x = np.minimum(freq_x, len_x - freq_x).astype(np.float32)
    freq_y = np.arange(len_y)
    freq_y = np.minimum(freq_y, len_y - freq_y).astype(np.float32)
    return 1.0 / (1.0 + (freq_x[:, None] ** 2 + freq_y[None, :] ** 2) / SCREEN)


def occupation(energy):
    return 1.0 / (1.0 + jnp.exp((energy - FERMI) / SMEAR))


def kernel(
    n_kx,
    n_ky,
    states,
    energies_in,
    reorder,
    external,
    along_y,
    along_x,
    back_x,
    back_y,
    screen,
    response_out,
    density_out,
    near,
    turned,
    energy,
    potential,
    bare,
    dense,
    wide,
    stage,
    outgoing,
    far,
    far_energy,
    wanted,
    order,
    weighted,
    part,
    gathered,
    crossed,
    whole,
    states_sem,
    order_send,
    order_recv,
    order_local,
    energy_send,
    energy_recv,
    rows_send,
    rows_recv,
    sum_send,
    sum_recv,
    cross_send,
    cross_recv,
    spread_send,
    spread_recv,
):
    grid, bands = near.shape
    nq = reorder.shape[0]
    piece = grid // PIECES
    lines = grid // LANES
    per = along_y.shape[0] // back_y.shape[0]
    share = piece // LANES
    kx = lax.axis_index("kx")
    ky = lax.axis_index("ky")

    def remote(source, target, send, recv, where):
        return pltpu.make_async_remote_copy(
            src_ref=source, dst_ref=target, send_sem=send, recv_sem=recv, device_id=where, device_id_type=MESH
        )

    load = pltpu.make_async_copy(states, near, states_sem)
    load.start()
    energy[...] = jnp.broadcast_to(energies_in[...].astype(jnp.float32), energy.shape)
    barrier = pltpu.get_barrier_semaphore()
    for step in range(1, n_kx):
        pl.semaphore_signal(barrier, inc=1, device_id={"kx": lax.rem(kx + step, n_kx)}, device_id_type=MESH)
    for step in range(1, n_ky):
        pl.semaphore_signal(barrier, inc=1, device_id={"ky": lax.rem(ky + step, n_ky)}, device_id_type=MESH)
    pl.semaphore_wait(barrier, n_kx + n_ky - 2)

    ahead = ({"kx": lax.rem(kx + 1, n_kx)}, {"ky": lax.rem(ky + 1, n_ky)})
    behind = ({"kx": lax.rem(kx + n_kx - 1, n_kx)}, {"ky": lax.rem(ky + n_ky - 1, n_ky)})

    orders = [
        remote(reorder.at[q], wanted.at[q], order_send.at[q], order_recv.at[q], ahead[q]) for q in range(nq)
    ]
    energies = [
        remote(energy, far_energy.at[q], energy_send.at[q], energy_recv.at[q], behind[q]) for q in range(nq)
    ]
    for q in range(nq):
        orders[q].start()
    for q in range(nq):
        energies[q].start()
    load.wait()
    wide[...] = near[...].astype(jnp.float32)
    locals_ = [pltpu.make_async_copy(wanted.at[q], order.at[q], order_local.at[q]) for q in range(nq)]
    for q in range(nq):
        orders[q].wait_recv()
        locals_[q].start()
    for q in range(nq):
        locals_[q].wait()

    def rows_copy(q, c):
        rows = pl.ds(pl.multiple_of(c * piece, piece), piece)
        return remote(
            outgoing.at[q, rows], far.at[q, rows], rows_send.at[q, c], rows_recv.at[q, c], behind[q]
        )

    def send_piece(c, carry):
        for q in range(nq):

            def some_rows(b, inner):
                first = pl.multiple_of(c * piece + b * ROWS, ROWS)
                for half in range(0, ROWS, 16):
                    picked = [wide[pl.ds(order[q, 0, first + half + r], 1), :] for r in range(16)]
                    for r in range(16):
                        stage[half + r : half + r + 1, :] = picked[r]
                outgoing[q, pl.ds(first, ROWS), :] = stage[...].astype(jnp.bfloat16)
                return inner

            lax.fori_loop(0, piece // ROWS, some_rows, 0)
            rows_copy(q, c).start()
        return carry

    lax.fori_loop(0, PIECES, send_piece, 0)

    def turn(c, carry):
        rows = pl.ds(pl.multiple_of(c * piece, piece), piece)
        turned[:, rows] = wide[rows, :].T.astype(jnp.bfloat16)
        return carry

    lax.fori_loop(0, PIECES, turn, 0)

    own = jnp.broadcast_to(energy[0:1, :], (bands, bands)).T
    weights = []
    for q in range(nq):
        energies[q].wait_recv()
        other = far_energy[q, 0:1, :]
        gap = other - own
        weights.append((occupation(own) - occupation(other)) * gap / (gap * gap + SMEAR * SMEAR))

    def bands_of(q, waits):
        def one(c, total):
            if waits:
                rows_copy(q, c).wait_recv()
            for t in range(share):
                cut = pl.ds(pl.multiple_of(c * piece + t * LANES, LANES), LANES)
                line = potential[pl.ds(q * lines + c * share + t, 1), :]
                weighted[:, t * LANES : (t + 1) * LANES] = (line * turned[:, cut].astype(jnp.float32)).astype(
                    jnp.bfloat16
                )
            rows = pl.ds(pl.multiple_of(c * piece, piece), piece)
            return total + jnp.dot(weighted[...], far[q, rows, :], preferred_element_type=jnp.float32)

        return lax.fori_loop(0, PIECES, one, jnp.zeros((bands, bands), jnp.float32))

    def density_of(q, low):
        def one(c, carry):
            rows = pl.ds(pl.multiple_of(c * piece, piece), piece)
            out = lax.dot_general(
                low, far[q, rows, :], (((1,), (1,)), ((), ())), preferred_element_type=jnp.float32
            )
            for t in range(share):
                cut = pl.ds(pl.multiple_of(c * piece + t * LANES, LANES), LANES)
                product = out[:, t * LANES : (t + 1) * LANES] * turned[:, cut].astype(jnp.float32)
                dense[pl.ds(q * lines + c * share + t, 1), :] = jnp.sum(product, axis=0, keepdims=True)
            return carry

        lax.fori_loop(0, PIECES, one, 0)

    scale = 1.0 / (math.sqrt(bands) * math.sqrt(n_kx * n_ky))

    def summed(rnd, total):
        part[rnd] = total.reshape(part.shape[1:])
        sends = []
        for d in range(1, n_ky):
            target = lax.rem(ky + d, n_ky)
            sends.append(
                remote(
                    part.at[rnd, target],
                    gathered.at[rnd, d],
                    sum_send.at[rnd, d],
                    sum_recv.at[rnd, d],
                    {"ky": target},
                )
            )
        for copy in sends:
            copy.start()
        mine = part[rnd, ky]
        for d, copy in enumerate(sends):
            copy.wait_recv()
            mine = mine + gathered[rnd, d + 1]
        crossed[rnd, kx] = mine
        crosses = []
        for d in range(1, n_kx):
            crosses.append(
                remote(
                    crossed.at[rnd, kx],
                    crossed.at[rnd, kx],
                    cross_send.at[rnd, d],
                    cross_recv.at[rnd, d],
                    {"kx": lax.rem(kx + d, n_kx)},
                )
            )
        for copy in crosses:
            copy.start()
        for copy in crosses:
            copy.wait_recv()
        mine = crossed[rnd, 0]
        for d in range(1, n_kx):
            mine = mine + crossed[rnd, d]
        whole[rnd, ky] = mine * scale
        spreads = []
        for d in range(1, n_ky):
            spreads.append(
                remote(
                    whole.at[rnd, ky],
                    whole.at[rnd, ky],
                    spread_send.at[rnd, d],
                    spread_recv.at[rnd, d],
                    {"ky": lax.rem(ky + d, n_ky)},
                )
            )
        for copy in spreads:
            copy.start()
        for copy in spreads:
            copy.wait_recv()
        return whole[rnd].reshape(total.shape), sends + crosses + spreads

    def exact(left, right):
        return jnp.dot(left, right, preferred_element_type=jnp.float32, precision=lax.Precision.HIGHEST)

    for t in range(lines):
        bare[t : t + 1, :] = external[:, t * LANES : (t + 1) * LANES]
    for q in range(nq):
        potential[q * lines : (q + 1) * lines, :] = bare[...]
    pending = []
    for rnd in range(ITERS):
        for q in reversed(range(nq)):
            mats = bands_of(q, rnd == 0) * (1.0 / math.sqrt(grid))
            response = weights[q] * mats
            if rnd + 1 == ITERS:
                response_out[q] = response.T
            density_of(q, response.astype(jnp.bfloat16))
        density, sends = summed(rnd, dense[...])
        pending = pending + sends
        if rnd + 1 < ITERS:
            mixed = exact(density, along_y[...])
            spectrum = exact(along_x[...], jnp.concatenate(jnp.split(mixed, per, axis=1), axis=0))
            filtered = exact(spectrum * screen[...], back_y[...])
            spread = exact(back_x[...], filtered)
            for q in range(nq):
                line = jnp.concatenate(
                    [spread[(q * per + b) * lines : (q * per + b + 1) * lines, :] for b in range(per)], axis=1
                )
                potential[q * lines : (q + 1) * lines, :] = bare[...] + line
    density_out[...] = density

    for q in range(nq):
        orders[q].wait_send()
        energies[q].wait_send()

    def drain(c, carry):
        for q in range(nq):
            rows_copy(q, c).wait_send()
        return carry

    lax.fori_loop(0, PIECES, drain, 0)
    for copy in pending:
        copy.wait_send()


def shards(n_kx, n_ky, states, energies, external, reorder):
    orbital = states[0]
    grid, bands = orbital.shape
    nq = reorder.shape[0]
    len_y = grid // GX
    lines = grid // LANES
    per = LANES // len_y
    hartley_x = hartley_table(GX)
    hartley_y = hartley_table(len_y)
    every_q = np.eye(nq, dtype=np.float32)
    cut_x = hartley_x.reshape(GX, lines, per)
    along_y = jnp.asarray(np.kron(np.eye(per, dtype=np.float32), hartley_y))
    along_x = jnp.asarray(np.einsum("qs,ptb->qpbst", every_q, cut_x).reshape(nq * GX, per * nq * lines))
    back_x = jnp.asarray(np.einsum("qs,ptb->qbtsp", every_q, cut_x).reshape(nq * per * lines, nq * GX))
    back_y = jnp.asarray(hartley_y)
    screen = jnp.asarray(np.tile(screening(GX, len_y), (nq, 1)).astype(np.float32))
    tall = nq * lines // n_ky
    vmem = pl.BlockSpec(memory_space=pltpu.VMEM)
    raw = pl.BlockSpec(memory_space=pl.ANY)
    dma = pltpu.SemaphoreType.DMA
    response, density = pl.pallas_call(
        functools.partial(kernel, n_kx, n_ky),
        out_shape=(
            jax.ShapeDtypeStruct((nq, bands, bands), jnp.float32),
            jax.ShapeDtypeStruct((nq * lines, LANES), jnp.float32),
        ),
        in_specs=[raw, vmem, raw] + [vmem] * 6,
        out_specs=(vmem, vmem),
        scratch_shapes=[
            pltpu.VMEM((grid, bands), jnp.bfloat16),
            pltpu.VMEM((bands, grid), jnp.bfloat16),
            pltpu.VMEM((8, bands), jnp.float32),
            pltpu.VMEM((nq * lines, LANES), jnp.float32),
            pltpu.VMEM((lines, LANES), jnp.float32),
            pltpu.VMEM((nq * lines, LANES), jnp.float32),
            pltpu.VMEM((grid, bands), jnp.float32),
            pltpu.VMEM((ROWS, bands), jnp.float32),
            pltpu.VMEM((nq, grid, bands), jnp.bfloat16),
            pltpu.VMEM((nq, grid, bands), jnp.bfloat16),
            pltpu.VMEM((nq, 8, bands), jnp.float32),
            pltpu.VMEM((nq, 1, grid), jnp.int32),
            pltpu.SMEM((nq, 1, grid), jnp.int32),
            pltpu.VMEM((bands, grid // PIECES), jnp.bfloat16),
            pltpu.VMEM((ITERS, n_ky, tall, LANES), jnp.float32),
            pltpu.VMEM((ITERS, n_ky, tall, LANES), jnp.float32),
            pltpu.VMEM((ITERS, n_kx, tall, LANES), jnp.float32),
            pltpu.VMEM((ITERS, n_ky, tall, LANES), jnp.float32),
            dma(()),
            dma((nq,)),
            dma((nq,)),
            dma((nq,)),
            dma((nq,)),
            dma((nq,)),
            dma((nq, PIECES)),
            dma((nq, PIECES)),
            dma((ITERS, n_ky)),
            dma((ITERS, n_ky)),
            dma((ITERS, n_kx)),
            dma((ITERS, n_kx)),
            dma((ITERS, n_ky)),
            dma((ITERS, n_ky)),
        ],
        compiler_params=pltpu.CompilerParams(
            collective_id=0, has_side_effects=True, vmem_limit_bytes=60 * 2**20
        ),
        cost_estimate=pl.CostEstimate(flops=2**31, bytes_accessed=2**23, transcendentals=2**16),
    )(orbital, energies, reorder, external, along_y, along_x, back_x, back_y, screen)
    density = density.reshape(nq, 1, grid)
    return (response[None, :, None], density)


def solution(mesh):
    return jax.shard_map(
        functools.partial(shards, mesh.shape["kx"], mesh.shape["ky"]),
        mesh=mesh,
        in_specs=(
            P(("kx", "ky"), None, None),
            P(("kx", "ky"), None),
            P(),
            P(None, ("kx", "ky"), None),
        ),
        out_specs=(P(("kx", "ky"), None, None, None, None), P()),
        check_vma=False,
    )
```

```python
import functools
import math

import jax
import jax.numpy as jnp
import numpy as np
from jax import lax
from jax.experimental import pallas as pl
from jax.experimental.pallas import tpu as pltpu
from jax.sharding import PartitionSpec as P

GX = 64
ITERS = 2


SMEAR = 0.5
FERMI = 0.0
SCREEN = 4.0
PIECES = 8
ROWS = 32
LANES = 128
MESH = pl.DeviceIdType.MESH


def hartley_table(length):
    positions = np.arange(length)
    angles = (positions[:, None] * positions[None, :] % length) * (2.0 * math.pi / length)
    return ((np.cos(angles) + np.sin(angles)) / math.sqrt(length)).astype(np.float32)


def screening(len_x, len_y):
    freq_x = np.arange(len_x)
    freq_x = np.minimum(freq_x, len_x - freq_x).astype(np.float32)
    freq_y = np.arange(len_y)
    freq_y = np.minimum(freq_y, len_y - freq_y).astype(np.float32)
    return 1.0 / (1.0 + (freq_x[:, None] ** 2 + freq_y[None, :] ** 2) / SCREEN)


def occupation(energy):
    return 1.0 / (1.0 + jnp.exp((energy - FERMI) / SMEAR))


def kernel(
    n_kx,
    n_ky,
    states,
    energies_in,
    reorder,
    external,
    along_y,
    along_x,
    back_x,
    back_y,
    screen,
    response_out,
    density_out,
    near,
    turned,
    energy,
    potential,
    bare,
    dense,
    wide,
    stage,
    outgoing,
    far,
    far_energy,
    wanted,
    order,
    weighted,
    part,
    gathered,
    crossed,
    whole,
    states_sem,
    order_send,
    order_recv,
    order_local,
    energy_send,
    energy_recv,
    rows_send,
    rows_recv,
    sum_send,
    sum_recv,
    cross_send,
    cross_recv,
    spread_send,
    spread_recv,
):
    grid, bands = near.shape
    nq = reorder.shape[0]
    piece = grid // PIECES
    lines = grid // LANES
    per = along_y.shape[0] // back_y.shape[0]
    share = piece // LANES
    kx = lax.axis_index("kx")
    ky = lax.axis_index("ky")

    def remote(source, target, send, recv, where):
        return pltpu.make_async_remote_copy(
            src_ref=source, dst_ref=target, send_sem=send, recv_sem=recv, device_id=where, device_id_type=MESH
        )

    load = pltpu.make_async_copy(states, near, states_sem)
    load.start()
    energy[...] = jnp.broadcast_to(energies_in[...].astype(jnp.float32), energy.shape)
    barrier = pltpu.get_barrier_semaphore()
    for step in range(1, n_kx):
        pl.semaphore_signal(barrier, inc=1, device_id={"kx": lax.rem(kx + step, n_kx)}, device_id_type=MESH)
    for step in range(1, n_ky):
        pl.semaphore_signal(barrier, inc=1, device_id={"ky": lax.rem(ky + step, n_ky)}, device_id_type=MESH)
    pl.semaphore_wait(barrier, n_kx + n_ky - 2)

    ahead = ({"kx": lax.rem(kx + 1, n_kx)}, {"ky": lax.rem(ky + 1, n_ky)})
    behind = ({"kx": lax.rem(kx + n_kx - 1, n_kx)}, {"ky": lax.rem(ky + n_ky - 1, n_ky)})

    orders = [
        remote(reorder.at[q], wanted.at[q], order_send.at[q], order_recv.at[q], ahead[q]) for q in range(nq)
    ]
    energies = [
        remote(energy, far_energy.at[q], energy_send.at[q], energy_recv.at[q], behind[q]) for q in range(nq)
    ]
    for q in range(nq):
        orders[q].start()
    for q in range(nq):
        energies[q].start()
    load.wait()
    wide[...] = near[...].astype(jnp.float32)
    locals_ = [pltpu.make_async_copy(wanted.at[q], order.at[q], order_local.at[q]) for q in range(nq)]
    for q in range(nq):
        orders[q].wait_recv()
        locals_[q].start()
    for q in range(nq):
        locals_[q].wait()

    def rows_copy(q, c):
        rows = pl.ds(pl.multiple_of(c * piece, piece), piece)
        return remote(
            outgoing.at[q, rows], far.at[q, rows], rows_send.at[q, c], rows_recv.at[q, c], behind[q]
        )

    def send_piece(c, carry):
        for q in range(nq):

            def some_rows(b, inner):
                first = pl.multiple_of(c * piece + b * ROWS, ROWS)
                for half in range(0, ROWS, 16):
                    picked = [wide[pl.ds(order[q, 0, first + half + r], 1), :] for r in range(16)]
                    for r in range(16):
                        stage[half + r : half + r + 1, :] = picked[r]
                outgoing[q, pl.ds(first, ROWS), :] = stage[...].astype(jnp.bfloat16)
                return inner

            lax.fori_loop(0, piece // ROWS, some_rows, 0)
            rows_copy(q, c).start()
        return carry

    lax.fori_loop(0, PIECES, send_piece, 0)

    def turn(c, carry):
        rows = pl.ds(pl.multiple_of(c * piece, piece), piece)
        turned[:, rows] = wide[rows, :].T.astype(jnp.bfloat16)
        return carry

    lax.fori_loop(0, PIECES, turn, 0)

    own = jnp.broadcast_to(energy[0:1, :], (bands, bands)).T
    weights = []
    for q in range(nq):
        energies[q].wait_recv()
        other = far_energy[q, 0:1, :]
        gap = other - own
        weights.append((occupation(own) - occupation(other)) * gap / (gap * gap + SMEAR * SMEAR))

    def bands_of(q, waits):
        def one(c, total):
            if waits:
                rows_copy(q, c).wait_recv()
            for t in range(share):
                cut = pl.ds(pl.multiple_of(c * piece + t * LANES, LANES), LANES)
                line = potential[pl.ds(q * lines + c * share + t, 1), :]
                weighted[:, t * LANES : (t + 1) * LANES] = (line * turned[:, cut].astype(jnp.float32)).astype(
                    jnp.bfloat16
                )
            rows = pl.ds(pl.multiple_of(c * piece, piece), piece)
            return total + jnp.dot(weighted[...], far[q, rows, :], preferred_element_type=jnp.float32)

        return lax.fori_loop(0, PIECES, one, jnp.zeros((bands, bands), jnp.float32), unroll=True)

    def density_of(q, low):
        def one(c, carry):
            rows = pl.ds(pl.multiple_of(c * piece, piece), piece)
            out = lax.dot_general(
                low, far[q, rows, :], (((1,), (1,)), ((), ())), preferred_element_type=jnp.float32
            )
            for t in range(share):
                cut = pl.ds(pl.multiple_of(c * piece + t * LANES, LANES), LANES)
                product = out[:, t * LANES : (t + 1) * LANES] * turned[:, cut].astype(jnp.float32)
                dense[pl.ds(q * lines + c * share + t, 1), :] = jnp.sum(product, axis=0, keepdims=True)
            return carry

        lax.fori_loop(0, PIECES, one, 0, unroll=True)

    scale = 1.0 / (math.sqrt(bands) * math.sqrt(n_kx * n_ky))

    def summed(rnd, total):
        part[rnd] = total.reshape(part.shape[1:])
        sends = []
        for d in range(1, n_ky):
            target = lax.rem(ky + d, n_ky)
            sends.append(
                remote(
                    part.at[rnd, target],
                    gathered.at[rnd, d],
                    sum_send.at[rnd, d],
                    sum_recv.at[rnd, d],
                    {"ky": target},
                )
            )
        for copy in sends:
            copy.start()
        mine = part[rnd, ky]
        for d, copy in enumerate(sends):
            copy.wait_recv()
            mine = mine + gathered[rnd, d + 1]
        crossed[rnd, kx] = mine
        crosses = []
        for d in range(1, n_kx):
            crosses.append(
                remote(
                    crossed.at[rnd, kx],
                    crossed.at[rnd, kx],
                    cross_send.at[rnd, d],
                    cross_recv.at[rnd, d],
                    {"kx": lax.rem(kx + d, n_kx)},
                )
            )
        for copy in crosses:
            copy.start()
        for copy in crosses:
            copy.wait_recv()
        mine = crossed[rnd, 0]
        for d in range(1, n_kx):
            mine = mine + crossed[rnd, d]
        whole[rnd, ky] = mine * scale
        spreads = []
        for d in range(1, n_ky):
            spreads.append(
                remote(
                    whole.at[rnd, ky],
                    whole.at[rnd, ky],
                    spread_send.at[rnd, d],
                    spread_recv.at[rnd, d],
                    {"ky": lax.rem(ky + d, n_ky)},
                )
            )
        for copy in spreads:
            copy.start()
        for copy in spreads:
            copy.wait_recv()
        return whole[rnd].reshape(total.shape), sends + crosses + spreads

    def exact(left, right):
        return jnp.dot(left, right, preferred_element_type=jnp.float32, precision=lax.Precision.HIGHEST)

    for t in range(lines):
        bare[t : t + 1, :] = external[:, t * LANES : (t + 1) * LANES]
    for q in range(nq):
        potential[q * lines : (q + 1) * lines, :] = bare[...]
    pending = []
    for rnd in range(ITERS):
        for q in reversed(range(nq)):
            mats = bands_of(q, rnd == 0) * (1.0 / math.sqrt(grid))
            response = weights[q] * mats
            if rnd + 1 == ITERS:
                response_out[q] = response.T
            density_of(q, response.astype(jnp.bfloat16))
        density, sends = summed(rnd, dense[...])
        pending = pending + sends
        if rnd + 1 < ITERS:
            mixed = exact(density, along_y[...])
            spectrum = exact(along_x[...], jnp.concatenate(jnp.split(mixed, per, axis=1), axis=0))
            filtered = exact(spectrum * screen[...], back_y[...])
            spread = exact(back_x[...], filtered)
            for q in range(nq):
                line = jnp.concatenate(
                    [spread[(q * per + b) * lines : (q * per + b + 1) * lines, :] for b in range(per)], axis=1
                )
                potential[q * lines : (q + 1) * lines, :] = bare[...] + line
    density_out[...] = density

    for q in range(nq):
        orders[q].wait_send()
        energies[q].wait_send()

    def drain(c, carry):
        for q in range(nq):
            rows_copy(q, c).wait_send()
        return carry

    lax.fori_loop(0, PIECES, drain, 0)
    for copy in pending:
        copy.wait_send()


def shards(n_kx, n_ky, states, energies, external, reorder):
    orbital = states[0]
    grid, bands = orbital.shape
    nq = reorder.shape[0]
    len_y = grid // GX
    lines = grid // LANES
    per = LANES // len_y
    hartley_x = hartley_table(GX)
    hartley_y = hartley_table(len_y)
    every_q = np.eye(nq, dtype=np.float32)
    cut_x = hartley_x.reshape(GX, lines, per)
    along_y = jnp.asarray(np.kron(np.eye(per, dtype=np.float32), hartley_y))
    along_x = jnp.asarray(np.einsum("qs,ptb->qpbst", every_q, cut_x).reshape(nq * GX, per * nq * lines))
    back_x = jnp.asarray(np.einsum("qs,ptb->qbtsp", every_q, cut_x).reshape(nq * per * lines, nq * GX))
    back_y = jnp.asarray(hartley_y)
    screen = jnp.asarray(np.tile(screening(GX, len_y), (nq, 1)).astype(np.float32))
    tall = nq * lines // n_ky
    vmem = pl.BlockSpec(memory_space=pltpu.VMEM)
    raw = pl.BlockSpec(memory_space=pl.ANY)
    dma = pltpu.SemaphoreType.DMA
    response, density = pl.pallas_call(
        functools.partial(kernel, n_kx, n_ky),
        out_shape=(
            jax.ShapeDtypeStruct((nq, bands, bands), jnp.float32),
            jax.ShapeDtypeStruct((nq * lines, LANES), jnp.float32),
        ),
        in_specs=[raw, vmem, raw] + [vmem] * 6,
        out_specs=(vmem, vmem),
        scratch_shapes=[
            pltpu.VMEM((grid, bands), jnp.bfloat16),
            pltpu.VMEM((bands, grid), jnp.bfloat16),
            pltpu.VMEM((8, bands), jnp.float32),
            pltpu.VMEM((nq * lines, LANES), jnp.float32),
            pltpu.VMEM((lines, LANES), jnp.float32),
            pltpu.VMEM((nq * lines, LANES), jnp.float32),
            pltpu.VMEM((grid, bands), jnp.float32),
            pltpu.VMEM((ROWS, bands), jnp.float32),
            pltpu.VMEM((nq, grid, bands), jnp.bfloat16),
            pltpu.VMEM((nq, grid, bands), jnp.bfloat16),
            pltpu.VMEM((nq, 8, bands), jnp.float32),
            pltpu.VMEM((nq, 1, grid), jnp.int32),
            pltpu.SMEM((nq, 1, grid), jnp.int32),
            pltpu.VMEM((bands, grid // PIECES), jnp.bfloat16),
            pltpu.VMEM((ITERS, n_ky, tall, LANES), jnp.float32),
            pltpu.VMEM((ITERS, n_ky, tall, LANES), jnp.float32),
            pltpu.VMEM((ITERS, n_kx, tall, LANES), jnp.float32),
            pltpu.VMEM((ITERS, n_ky, tall, LANES), jnp.float32),
            dma(()),
            dma((nq,)),
            dma((nq,)),
            dma((nq,)),
            dma((nq,)),
            dma((nq,)),
            dma((nq, PIECES)),
            dma((nq, PIECES)),
            dma((ITERS, n_ky)),
            dma((ITERS, n_ky)),
            dma((ITERS, n_kx)),
            dma((ITERS, n_kx)),
            dma((ITERS, n_ky)),
            dma((ITERS, n_ky)),
        ],
        compiler_params=pltpu.CompilerParams(
            collective_id=0, has_side_effects=True, vmem_limit_bytes=60 * 2**20
        ),
        cost_estimate=pl.CostEstimate(flops=2**31, bytes_accessed=2**23, transcendentals=2**16),
    )(orbital, energies, reorder, external, along_y, along_x, back_x, back_y, screen)
    density = density.reshape(nq, 1, grid)
    return (response[None, :, None], density)


def solution(mesh):
    return jax.shard_map(
        functools.partial(shards, mesh.shape["kx"], mesh.shape["ky"]),
        mesh=mesh,
        in_specs=(
            P(("kx", "ky"), None, None),
            P(("kx", "ky"), None),
            P(),
            P(None, ("kx", "ky"), None),
        ),
        out_specs=(P(("kx", "ky"), None, None, None, None), P()),
        check_vma=False,
    )
```
